1024 devices in a mesh: section: 16 (over y, core), expert: 64 (over z, x).
Axes of the slice: x: 4, y: 8, z: 16, core: 2. Of those that a mesh axis runs over, the one named last changes fastest.
Arguments:
- held: bfloat16 [16, 8192, 3584], P('section', 'expert'), may hold values from -0.59765625 to 0.59765625
- incoming: bfloat16 [1, 8192, 3584], P(None, 'expert'), may hold values from -0.59765625 to 0.59765625
- route_ids: int32 [2, 16, 8192, 8], P(None, 'section', 'expert'), may hold values from 0 to 255, all different within a row; in each aligned block of 128 rows (0 to 127, 128 to 255, ..., all dimensions but the last counted through in order) at most 4 rows name the same one
- gain: bfloat16 [16, 3584], P('section'), may hold values from 0.099609375 to 1.8984375
- router: bfloat16 [16, 3584, 256], P('section'), may hold values from -0.09375 to 0.09375
- w_gate: bfloat16 [16, 4096, 3584], P('section', 'expert'), may hold values from -0.09375 to 0.09375
- w_up: bfloat16 [16, 4096, 3584], P('section', 'expert'), may hold values from -0.09375 to 0.09375
- w_down: bfloat16 [16, 4096, 3584], P('section', 'expert'), may hold values from -0.5 to 0.5
Outputs:
- layer_out: bfloat16 [16, 8192, 3584], P('section', 'expert')
The draws below stay inside these ranges and needn't reach their ends.
Inputs may be any that keep to these rules, and one draw needn't show every extreme that they name: `route_ids`: each row names 8 different experts. Within the 128 rows of one device at one tick and section, no expert is named by more than 4 rows; some expert is named by exactly 4 rows in some such blocks.
All inputs are finite; a program needn't handle non-finite values.
Results may differ from the reference program's by a relative error of at most 0.0073.
Values may be sent and summed in bfloat16 or wider, within the bound.
A program may use at most 32 MiB of HBM per device.

```python
import math
import jax
import jax.numpy as jnp
import numpy as np
from jax import lax

D = 3584
FF_WIN = 1024
EXPERTS = 256
TOP = 8
TICKS = 2
TOK_DEV = 128
GROUP = 16
FF_DEV = 64
EXP_FLY = 4
NSTG = 16
TOKENS = 8192
CAP = 4
N_EXPERT = 64


def block_levels(key, shape, pieces, least, high):
    level = 1.0
    for position, parts in pieces:
        steps = jax.random.uniform(jax.random.fold_in(jax.random.fold_in(key, 6), position), (parts,), jnp.float32, least / len(pieces), high / len(pieces))
        level = level * jnp.repeat(jnp.exp(steps), shape[position] // parts).reshape((-1,) + (1,) * (len(shape) - 1 - position))
    return level


def assign_block(key, own, number, rows, number_of, top, most, skew):
    ranking = jax.random.permutation(key, number_of)
    heavy_load, ordinary = portions_of(number_of, rows * top, most, skew, True), portions_of(number_of, rows * top, most, skew, False)
    places = jnp.arange(number_of)

    def named(lengths, offset_by):
        used = int((lengths > 0).sum())
        fixed = max(1, used // 4)
        shifted = fixed + (places - fixed + offset_by * (used - fixed)) % max(1, number_of - fixed)
        return jnp.zeros((number_of,), jnp.int32).at[ranking[jnp.where(places < fixed, places, shifted)]].set(jnp.asarray(lengths, jnp.int32))

    lengths = jnp.where(number % 4 == 0, named(heavy_load, number // 4), named(ordinary, number - number // 4 - 1))
    mixed = jax.random.permutation(jax.random.fold_in(own, 3), number_of)
    giver, receiver = mixed[0:number_of // 2 * 2:2], mixed[1:number_of // 2 * 2:2]
    room = jnp.minimum(lengths[giver] - 1, most - lengths[receiver]) // 2
    room = jnp.where((giver == ranking[0]) | (receiver == ranking[0]) | (lengths[receiver] == 0), 0, jnp.maximum(room, 0))
    shifted = jax.random.randint(jax.random.fold_in(own, 4), (number_of // 2,), 0, 1 << 20) % (room + 1)
    lengths = lengths.at[giver].add(-shifted).at[receiver].add(shifted)
    labels = jnp.searchsorted(jnp.cumsum(lengths), jnp.arange(rows * top), side="right").astype(jnp.int32)
    listing = labels.reshape(top, rows).T
    listing = listing[jax.random.permutation(jax.random.fold_in(own, 1), rows)]
    offset_by = jax.random.randint(jax.random.fold_in(own, 2), (rows, 1), 0, top)
    return jnp.take_along_axis(listing, (jnp.arange(top)[None, :] + offset_by) % top, axis=1)


def portions_of(number_of, total, bound, lean, full):
    loads = [(1 << 20) // math.isqrt(grade ** lean) + 1 for grade in range(1, number_of + 1)]
    largest = bound if full else min(bound, max(-(-total // number_of), total * loads[0] // sum(loads)))
    least = 1 if total - largest >= number_of - 1 else 0
    counts, rest = [largest] + [least] * (number_of - 1), total - largest - least * (number_of - 1)
    while rest > 0:
        free = [i for i in range(1, number_of) if counts[i] < largest] or [i for i in range(1, number_of) if counts[i] < bound]
        whole, left = sum([loads[i] for i in free]), rest
        for i in free:
            addition = min(bound - counts[i], max(1, left * loads[i] // whole), rest)
            counts[i] = counts[i] + addition
            rest = rest - addition
    return np.array(counts)


def gaussian(key, shape, deviation, most, shards=(), kind=jnp.bfloat16):
    entries = deviation * jax.random.normal(key, shape, jnp.float32)
    if shards:
        entries = entries * block_levels(key, shape, shards, -0.22, 0.18)
    return jnp.clip(entries, -most, most).astype(kind)


def setup_inputs(seed: int = 0) -> dict:
    key_of = jax.random.split(jax.random.key(seed), 9)
    held = gaussian(key_of[0], (NSTG, TOKENS, D), 0.1, 0.59765625, ((0, 16), (1, 64)))
    incoming = gaussian(key_of[1], (TICKS - 1, TOKENS, D), 0.1, 0.59765625, ((1, 64),))
    route_ids_keys = jax.random.split(jax.random.fold_in(key_of[2], 1), TICKS * NSTG * TOKENS // TOK_DEV)
    route_ids_turns = jax.random.permutation(jax.random.fold_in(key_of[2], 3), TICKS * NSTG * TOKENS // TOK_DEV)
    route_ids = jax.vmap(lambda own, number: assign_block(jax.random.fold_in(key_of[2], 2), own, number, TOK_DEV, EXPERTS, TOP, CAP, 2))(route_ids_keys, route_ids_turns).reshape((TICKS, NSTG, TOKENS, TOP))
    gain = jnp.clip(1.0 + 0.18 * jax.random.normal(key_of[3], (NSTG, D), jnp.float32), 0.099609375, 1.8984375).astype(jnp.bfloat16)
    router = gaussian(key_of[4], (NSTG, D, EXPERTS), D ** -0.5, 0.09375, ((0, 16),))
    w_gate = gaussian(key_of[5], (NSTG, EXP_FLY * FF_WIN, D), D ** -0.5, 0.09375, ((0, 16), (1, 64)))
    w_up = gaussian(key_of[6], (NSTG, EXP_FLY * FF_WIN, D), D ** -0.5, 0.09375, ((0, 16), (1, 64)))
    w_down = gaussian(key_of[7], (NSTG, EXP_FLY * FF_WIN, D), (FF_WIN // 8) ** -0.5, 0.5, ((0, 16), (1, 64)))
    return {"held": held, "incoming": incoming, "route_ids": route_ids, "gain": gain, "router": router, "w_gate": w_gate, "w_up": w_up, "w_down": w_down}


route_scale = 2.5

def expert_ffn(rows, gate_w, up_w, down_w):
    dims = (((1,), (1,)), ((), ()))
    gate = lax.dot_general(rows, gate_w, dims, preferred_element_type=jnp.float32)
    upper = lax.dot_general(rows, up_w, dims, preferred_element_type=jnp.float32)
    hidden = (jax.nn.silu(gate) * upper).astype(jnp.bfloat16)
    count = rows.shape[0]
    hidden_parts = hidden.astype(jnp.float32).reshape(count, GROUP, FF_DEV)
    down_parts = down_w.astype(jnp.float32).reshape(GROUP, FF_DEV, down_w.shape[1])
    partial_value = jnp.einsum('rgh,ghd->rgd', hidden_parts, down_parts).astype(jnp.bfloat16)
    partial_value = lax.optimization_barrier(partial_value)
    return lax.optimization_barrier(jnp.sum(partial_value.astype(jnp.float32), 1))

def route_layer(state, ids, gain_row, router_w, gate_all, up_all, down_all):
    x_val = state.astype(jnp.float32)
    normed = (x_val * lax.rsqrt(lax.optimization_barrier(jnp.mean(x_val * x_val, -1, keepdims=True)) + 1e-06) * gain_row.astype(jnp.float32)).astype(jnp.bfloat16)
    scores = jax.nn.sigmoid(jnp.dot(normed, router_w, preferred_element_type=jnp.float32))
    chosen = jnp.take_along_axis(scores, ids, axis=1)
    weights = route_scale * chosen / lax.optimization_barrier(jnp.sum(chosen, -1, keepdims=True))
    tokens = state.shape[0]
    most = N_EXPERT * CAP
    padded = jnp.concatenate([normed, jnp.zeros((1, normed.shape[1]), jnp.bfloat16)], 0)
    width = normed.shape[1]
    gate_set = gate_all.reshape(EXP_FLY, FF_WIN, width)
    up_set = up_all.reshape(EXP_FLY, FF_WIN, width)
    down_set = down_all.reshape(EXP_FLY, FF_WIN, width)

    def one_expert(carry, packed):
        number, gate_w, up_w, down_w = packed
        hit = ids == number
        taken = jnp.any(hit, -1)
        rows = jnp.nonzero(taken, size=most, fill_value=tokens)[0].astype(jnp.int32)
        row_weight = lax.optimization_barrier(jnp.sum(jnp.where(hit, weights, 0.0), -1))
        row_weight = jnp.concatenate([row_weight, jnp.zeros((1,), row_weight.dtype)], 0)
        output = expert_ffn(padded[rows], gate_w, up_w, down_w)
        carry = carry.at[rows].add(row_weight[rows][:, None] * output)
        return (carry, None)
    start = jnp.zeros((tokens + 1, width), jnp.float32)
    numbers = jnp.arange(EXP_FLY, dtype=jnp.int32)
    combined, unused = lax.scan(one_expert, start, (numbers, gate_set, up_set, down_set))
    return (x_val + combined[:tokens]).astype(jnp.bfloat16)

def reference(held, incoming, route_ids, gain, router, w_gate, w_up, w_down):
    state = held
    output = held
    for tick in range(TICKS):
        if tick > 0:
            state = jnp.concatenate([incoming[tick - 1][None], output[:-1]], 0)
        output = lax.map(lambda packed: route_layer(*packed), (state, route_ids[tick], gain, router, w_gate, w_up, w_down))
    return output
```

```python
import jax
import jax.numpy as jnp
from jax import lax
from jax.experimental import pallas as pl
from jax.experimental.pallas import tpu as pltpu
from jax.sharding import PartitionSpec as P

MESH = pl.DeviceIdType.MESH
F32 = jnp.float32
BF16 = jnp.bfloat16

SCALE = 2.5
D = 3584
TOK = 128
TOP = 8
CAP = 4
SLOTS = 16
UNITS = 64
NZ = 16
SUB = 4
DS = D // SUB
LB = DS // 128
EXPERTS = 256
NSEC = 16

S_LOCAL, S_WGU, S_WD, S_X, S_IDS, S_Y = 0, 1, 2, 3, 4, 5
S_TICK = 6
N_SEM = S_TICK + 12
L_X, L_IDS, L_GAIN, L_ROUTER, L_WGU, L_WD, L_OUT = range(7)


def nt(a, b):
    return lax.dot_general(a, b, (((1,), (1,)), ((), ())), preferred_element_type=F32)


def nn(a, b):
    return jnp.dot(a, b, preferred_element_type=F32)


def iota(shape, dim):
    return lax.broadcasted_iota(jnp.int32, shape, dim)


def swap_halves(a):
    return pltpu.roll(a, 4, a.ndim - 2)


def one_hot(flag):
    return jnp.where(flag, 1.0, 0.0).astype(BF16)


def halves(a):
    high = a.astype(BF16)
    low = (a - high.astype(F32)).astype(BF16)
    return jnp.concatenate([high, low], 0)


def placing(ids):
    ids_f = ids.astype(F32).astype(BF16)
    eye = one_hot(iota((TOP, TOP), 0) == iota((TOP, TOP), 1))
    ids_t = nt(eye, ids_f)
    expert_of = (iota((SLOTS, TOK), 0) // CAP).astype(F32)
    hit = jnp.zeros((SLOTS, TOK), F32)
    for k in range(TOP):
        hit = jnp.where(ids_t[k : k + 1, :] == expert_of, 1.0, hit)
    earlier = one_hot(iota((TOK, TOK), 0) < iota((TOK, TOK), 1))
    before = nn(hit.astype(BF16), earlier)
    turn = (iota((SLOTS, TOK), 0) % CAP).astype(F32)
    place = jnp.where(before == turn, hit, 0.0).astype(BF16)
    return place, nn(place, ids_f)


def normalize(comp, gain):
    mean = jnp.mean(comp * comp, -1, keepdims=True)
    return (comp * lax.rsqrt(mean + 1e-06) * gain).astype(BF16)


def slot_weights(normed, router, slot_ids):
    scores = jax.nn.sigmoid(nn(normed, router))
    lane = iota((SLOTS, EXPERTS), 1)
    lane_f = lane.astype(F32)
    picked = jnp.zeros((SLOTS, EXPERTS), F32)
    for k in range(TOP):
        picked = jnp.where(slot_ids[:, k : k + 1] == lane_f, 1.0, picked)
    total = jnp.sum(scores * picked, -1, keepdims=True)
    own = jnp.sum(
        jnp.where(lane == iota((SLOTS, EXPERTS), 0) // CAP, scores, 0.0), -1, keepdims=True
    )
    return SCALE * own / total


def kernel(
    held, incoming, ids, gain, router, wg, wu, wd, out,
    xv, xp, idv, idp, gv, rv, wgu, wdv,
    zsend, zrecv, xbuf, rsend, rrecv, guf, hbuf, osend, orecv, of, bsend, brecv,
    ysend, yrecv, b1, ov, comp_s, comp1_s, moe_s,
    loc, snd, rcv,
):
    sec = lax.axis_index("section")
    ex = lax.axis_index("expert")
    z, x = ex // SUB, ex % SUB
    e, zz = z // SUB, z % SUB

    def at_z(other):
        return {"expert": other * SUB + x}

    def at_x(other):
        return {"expert": z * SUB + other}

    after = {"section": (sec + 1) % NSEC}
    before = {"section": (sec + NSEC - 1) % NSEC}

    def local(src, dst, number):
        return pltpu.make_async_copy(src, dst, loc.at[number])

    def send(src, dst, number, device):
        pltpu.make_async_remote_copy(
            src_ref=src, dst_ref=dst, send_sem=snd.at[number], recv_sem=rcv.at[number],
            device_id=device, device_id_type=MESH,
        ).start()

    def arrived(ref, number):
        pltpu.make_async_copy(ref, ref, rcv.at[number]).wait()

    def sent(ref, number):
        pltpu.make_async_copy(ref, ref, snd.at[number]).wait()

    own = pl.ds(pl.multiple_of(zz * DS, 128), DS)
    starts = [
        local(held.at[0], xv, L_X),
        local(ids.at[:, 0], idv, L_IDS),
        local(gain, gv, L_GAIN),
        local(router.at[0], rv, L_ROUTER),
        local(wg.at[0, :, own], wgu.at[0, zz], L_WGU),
        local(wu.at[0, :, own], wgu.at[1, zz], L_WGU),
        local(wd.at[0, :, own], wdv.at[zz], L_WD),
    ]
    for copy in starts:
        copy.start()

    barrier = pltpu.get_barrier_semaphore()

    @pl.loop(1, NZ)
    def _(k):
        pl.semaphore_signal(barrier, inc=1, device_id=at_z((z + k) % NZ), device_id_type=MESH)

    for k in range(1, SUB):
        pl.semaphore_signal(barrier, inc=1, device_id=at_x((x + k) % SUB), device_id_type=MESH)
    pl.semaphore_signal(barrier, inc=1, device_id=after, device_id_type=MESH)
    pl.semaphore_signal(barrier, inc=1, device_id=before, device_id_type=MESH)
    pl.semaphore_wait(barrier, NZ - 1 + SUB - 1 + 2)

    for k in range(1, SUB):
        to = (zz + k) % SUB
        columns = pl.ds(pl.multiple_of(to * DS, 128), DS)
        send(wg.at[0, :, columns], wgu.at[0, zz], S_WGU, at_z(e * SUB + to))
        send(wu.at[0, :, columns], wgu.at[1, zz], S_WGU, at_z(e * SUB + to))

    local(ids.at[:, 0], idv, L_IDS).wait()
    place0, slot_ids0 = placing(idv[0])
    local(gain, gv, L_GAIN).wait()
    gain_row = gv[...].astype(F32)
    local(held.at[0], xv, L_X).wait()
    low4 = iota((1, 8, 128), 1) < 4

    def dispatch(tick, normed):
        rows = normed.astype(F32)
        for part in range(SUB):
            for w in range(2):
                pieces = [[] for _ in range(4)]
                for v in (2 * w, 2 * w + 1):
                    column = (part * LB + 2 * v) * 128
                    a = rows[:, column : column + 128].reshape(2, 8, 128)
                    if 2 * v + 1 < LB:
                        b = rows[:, column + 128 : column + 256].reshape(2, 8, 128)
                    else:
                        b = jnp.zeros((2, 8, 128), F32)
                    even = jnp.where(low4, a, swap_halves(b))
                    odd = jnp.where(low4, swap_halves(a), b)
                    for h in range(2):
                        pieces[2 * h].append(even[h])
                        pieces[2 * h + 1].append(odd[h])
                for n in range(4):
                    zsend[tick, n * SUB + part, 16 * w : 16 * w + 16, :] = jnp.concatenate(
                        pieces[n], 0
                    ).astype(BF16)
        number = S_TICK + 6 * tick

        @pl.loop(1, NZ)
        def _(k):
            to = (z + k) % NZ
            send(zsend.at[tick, to], zrecv.at[tick, z], number, at_z(to))

        zrecv[tick, z] = zsend[tick, z]

    def layer(tick, meanwhile):
        base = S_TICK + 6 * tick
        arrived(zrecv.at[tick, pl.ds(0, NZ - 1)], base)
        got = zrecv[tick].astype(F32).reshape(8, 2, 4, 8, 128)
        for v in range(4):
            a, b = got[:, 0, v], got[:, 1, v]
            even = jnp.where(low4, a, swap_halves(b))
            xbuf[tick, x, :, 2 * v * 128 : (2 * v + 1) * 128] = even.reshape(64, 128).astype(BF16)
            if 2 * v + 1 < LB:
                odd = jnp.where(low4, swap_halves(a), b)
                xbuf[tick, x, :, (2 * v + 1) * 128 : (2 * v + 2) * 128] = odd.reshape(64, 128).astype(BF16)
        for k in range(1, SUB):
            send(xbuf.at[tick, x], xbuf.at[tick, x], base + 1, at_x((x + k) % SUB))
        if tick == 0:
            local(wgu.at[:, zz], wgu.at[:, zz], L_WGU).wait()
            arrived(wgu.at[:, pl.ds(0, SUB - 1)], S_WGU)
        arrived(xbuf.at[tick, pl.ds(0, SUB - 1)], base + 1)
        sums = nt(xbuf[tick].reshape(256, DS), wgu[...].reshape(512, DS))
        sums = sums.reshape(SUB, 64, 512)
        rsend[tick] = sums.astype(BF16)
        guf[...] = sums
        for k in range(1, SUB):
            to = (zz + k) % SUB
            send(rsend.at[tick, to], rrecv.at[tick, zz], base + 2, at_z(e * SUB + to))
        arrived(rrecv.at[tick, pl.ds(0, SUB - 1)], base + 2)
        total = guf[zz]
        for k in range(1, SUB):
            total = total + rrecv[tick, (zz + k) % SUB].astype(F32)
        gate, upper = total[:, :256], total[:, 256:]
        hbuf[tick, zz] = (jax.nn.silu(gate) * upper).astype(BF16)
        for k in range(1, SUB):
            send(hbuf.at[tick, zz], hbuf.at[tick, zz], base + 3, at_z(e * SUB + (zz + k) % SUB))
        if tick == 0:
            local(wd.at[0, :, own], wdv.at[zz], L_WD).wait()
            arrived(wdv.at[pl.ds(0, SUB - 1)], S_WD)
        arrived(hbuf.at[tick, pl.ds(0, SUB - 1)], base + 3)
        product = nn(hbuf[tick].reshape(256, 256), wdv[...].reshape(256, DS))
        product = product.reshape(SUB, 64, DS)
        osend[tick] = product.astype(BF16)
        of[...] = product
        for k in range(1, SUB):
            to = (x + k) % SUB
            send(osend.at[tick, to], orecv.at[tick, x], base + 4, at_x(to))
        arrived(orecv.at[tick, pl.ds(0, SUB - 1)], base + 4)
        total = of[x]
        for k in range(1, SUB):
            total = total + orecv[tick, (x + k) % SUB].astype(F32)
        for w in range(2):
            evens, odds = [], []
            for v in (2 * w, 2 * w + 1):
                a = total[:, 2 * v * 128 : (2 * v + 1) * 128].reshape(8, 8, 128)
                if 2 * v + 1 < LB:
                    b = total[:, (2 * v + 1) * 128 : (2 * v + 2) * 128].reshape(8, 8, 128)
                else:
                    b = jnp.zeros((8, 8, 128), F32)
                evens.append(jnp.where(low4, a, swap_halves(b)))
                odds.append(jnp.where(low4, swap_halves(a), b))
            bsend[tick, :, 0, 16 * w : 16 * w + 16, :] = jnp.concatenate(evens, 1).astype(BF16)
            bsend[tick, :, 1, 16 * w : 16 * w + 16, :] = jnp.concatenate(odds, 1).astype(BF16)

        @pl.loop(1, NZ)
        def _(k):
            to = (z + k) % NZ
            send(bsend.at[tick, to // 2, to % 2], brecv.at[tick, z], base + 5, at_z(to))

        brecv[tick, z] = bsend[tick, z // 2, z % 2]
        meanwhile()
        arrived(brecv.at[tick, pl.ds(0, NZ - 1)], base + 5)
        for half in range(2):
            for part in range(SUB):
                first = brecv[tick, (2 * half) * SUB + part].astype(F32).reshape(4, 8, 128)
                second = brecv[tick, (2 * half + 1) * SUB + part].astype(F32).reshape(4, 8, 128)
                even = jnp.where(low4, first, swap_halves(second))
                odd = jnp.where(low4, swap_halves(first), second)
                for v in range(4):
                    column = (part * LB + 2 * v) * 128
                    moe_s[8 * half : 8 * half + 8, column : column + 128] = even[v]
                    if 2 * v + 1 < LB:
                        moe_s[8 * half : 8 * half + 8, column + 128 : column + 256] = odd[v]
        return moe_s[...]

    comp = nn(place0, xv[...])
    comp_s[...] = comp
    normed = normalize(comp, gain_row)
    dispatch(0, normed)
    for k in range(1, SUB):
        to = (zz + k) % SUB
        columns = pl.ds(pl.multiple_of(to * DS, 128), DS)
        send(wd.at[0, :, columns], wdv.at[zz], S_WD, at_z(e * SUB + to))

    @pl.when(sec == NSEC - 1)
    def _():
        send(incoming.at[0], xp, S_X, after)

    @pl.when(sec != NSEC - 1)
    def _():
        send(held.at[0], xp, S_X, after)

    send(idv.at[0], idp, S_IDS, after)
    local(router.at[0], rv, L_ROUTER).wait()
    weights0 = slot_weights(normed, rv[...], slot_ids0)
    same = nt(place0, place0).astype(BF16)
    same2 = jnp.concatenate([same, same], 1)
    place1, slot_ids1 = placing(idv[1])

    def prepare():
        arrived(idp, S_IDS)
        arrived(xp, S_X)
        prev, _ = placing(idp[...])
        lower = one_hot(iota((SLOTS, SLOTS), 1) < iota((SLOTS, SLOTS), 0))
        seen = nn(lower, prev)
        live = jnp.where(sec == 0, 0.0, 1.0)
        unique = jnp.where(seen == 0.0, prev.astype(F32), 0.0) * live
        touched = jnp.sum(unique, 0, keepdims=True)
        untouched = (place1.astype(F32) * (1.0 - touched)).astype(BF16)
        comp1_s[...] = nn(untouched, xp[...])

    moe = layer(0, prepare)
    y16 = comp_s[...] + nn(same2, halves(moe * weights0))
    ysend[...] = y16.astype(BF16)
    send(ysend, yrecv, S_Y, after)
    prev, _ = placing(idp[...])
    lower = one_hot(iota((SLOTS, SLOTS), 1) < iota((SLOTS, SLOTS), 0))
    live = jnp.where(sec == 0, 0.0, 1.0)
    unique = jnp.where(nn(lower, prev) == 0.0, prev.astype(F32), 0.0) * live
    unique = unique.astype(BF16)
    moved = nt(place1, unique).astype(BF16)
    eye = one_hot(iota((TOK, TOK), 0) == iota((TOK, TOK), 1))
    scatter = nt(eye, unique).astype(BF16)
    combine = nt(eye, jnp.concatenate([place1, place1], 0)).astype(BF16)
    kept = 1.0 - jnp.sum(scatter.astype(F32), 1, keepdims=True)
    arrived(yrecv, S_Y)
    normed = normalize(comp1_s[...] + nn(moved, yrecv[...]), gain_row)
    dispatch(1, normed)
    weights1 = slot_weights(normed, rv[...], slot_ids1)

    def block():
        for part in range(SUB):
            columns = slice(part * DS, (part + 1) * DS)
            b1[:, columns] = xp[:, columns].astype(F32) * kept + nn(scatter, yrecv[:, columns])

    moe = layer(1, block)
    summands = halves(moe * weights1)
    outs = []
    for part in range(SUB):
        columns = slice(part * DS, (part + 1) * DS)
        ov[:, columns] = (b1[:, columns] + nn(combine, summands[:, columns])).astype(BF16)
        copy = local(ov.at[:, columns], out.at[0, :, columns], L_OUT + part)
        copy.start()
        outs.append(copy)
    sent(wgu.at[:, pl.ds(0, SUB - 1)], S_WGU)
    sent(wdv.at[pl.ds(0, SUB - 1)], S_WD)
    sent(xp, S_X)
    sent(idp, S_IDS)
    sent(yrecv, S_Y)
    for tick in range(2):
        base = S_TICK + 6 * tick
        sent(zrecv.at[tick, pl.ds(0, NZ - 1)], base)
        sent(xbuf.at[tick, pl.ds(0, SUB - 1)], base + 1)
        sent(rrecv.at[tick, pl.ds(0, SUB - 1)], base + 2)
        sent(hbuf.at[tick, pl.ds(0, SUB - 1)], base + 3)
        sent(orecv.at[tick, pl.ds(0, SUB - 1)], base + 4)
        sent(brecv.at[tick, pl.ds(0, NZ - 1)], base + 5)
    for copy in outs:
        copy.wait()


def body(held, incoming, route_ids, gain, router, w_gate, w_up, w_down):
    any_space = pl.BlockSpec(memory_space=pl.ANY)
    vm = pltpu.VMEM
    return pl.pallas_call(
        kernel,
        out_shape=jax.ShapeDtypeStruct((1, TOK, D), BF16),
        in_specs=[any_space] * 8,
        out_specs=any_space,
        scratch_shapes=[
            vm((TOK, D), BF16),
            vm((TOK, D), BF16),
            vm((2, TOK, TOP), jnp.int32),
            vm((TOK, TOP), jnp.int32),
            vm((1, D), BF16),
            vm((D, EXPERTS), BF16),
            vm((2, SUB, UNITS, DS), BF16),
            vm((SUB, UNITS, DS), BF16),
            vm((2, NZ, 32, 128), BF16),
            vm((2, NZ, 32, 128), BF16),
            vm((2, SUB, 64, DS), BF16),
            vm((2, SUB, 64, 512), BF16),
            vm((2, SUB, 64, 512), BF16),
            vm((SUB, 64, 512), F32),
            vm((2, SUB, 64, 256), BF16),
            vm((2, SUB, 64, DS), BF16),
            vm((2, SUB, 64, DS), BF16),
            vm((SUB, 64, DS), F32),
            vm((2, 8, 2, 32, 128), BF16),
            vm((2, NZ, 32, 128), BF16),
            vm((SLOTS, D), BF16),
            vm((SLOTS, D), BF16),
            vm((TOK, D), F32),
            vm((TOK, D), BF16),
            vm((SLOTS, D), F32),
            vm((SLOTS, D), F32),
            vm((SLOTS, D), F32),
            pltpu.SemaphoreType.DMA((L_OUT + SUB,)),
            pltpu.SemaphoreType.DMA((N_SEM,)),
            pltpu.SemaphoreType.DMA((N_SEM,)),
        ],
        compiler_params=pltpu.CompilerParams(
            collective_id=0, has_side_effects=True, vmem_limit_bytes=48 * 1024 * 1024
        ),
    )(held, incoming, route_ids, gain, router, w_gate, w_up, w_down)


def solution(mesh):
    return jax.shard_map(
        body,
        mesh=mesh,
        in_specs=(
            P("section", "expert", None),
            P(None, "expert", None),
            P(None, "section", "expert", None),
            P("section", None),
            P("section", None, None),
            P("section", "expert", None),
            P("section", "expert", None),
            P("section", "expert", None),
        ),
        out_specs=P("section", "expert", None),
        check_vma=False,
    )
```

```python
import jax
import jax.numpy as jnp
from jax import lax
from jax.experimental import pallas as pl
from jax.experimental.pallas import tpu as pltpu
from jax.sharding import PartitionSpec as P

MESH = pl.DeviceIdType.MESH
F32 = jnp.float32
BF16 = jnp.bfloat16

SCALE = 2.5
D = 3584
TOK = 128
TOP = 8
CAP = 4
SLOTS = 16
UNITS = 64
NZ = 16
SUB = 4
DS = D // SUB
LB = DS // 128
EXPERTS = 256
HALF = (0, 512), (512, DS)
BLOCKS = (0, 4), (4, LB)
NSEC = 16

S_WGU, S_WD, S_X, S_IDS, S_Y = 1, 2, 3, 4, 5
S_TICK = 7
PER_TICK = 12
N_SEM = S_TICK + 2 * PER_TICK
L_X, L_IDS, L_GAIN, L_ROUTER, L_WGU, L_WD, L_OUT = range(7)


def nt(a, b):
    return lax.dot_general(a, b, (((1,), (1,)), ((), ())), preferred_element_type=F32)


def nn(a, b):
    return jnp.dot(a, b, preferred_element_type=F32)


def iota(shape, dim):
    return lax.broadcasted_iota(jnp.int32, shape, dim)


def swap_halves(a):
    return pltpu.roll(a, 4, a.ndim - 2)


def one_hot(flag):
    return jnp.where(flag, 1.0, 0.0).astype(BF16)


def halves(a):
    high = a.astype(BF16)
    low = (a - high.astype(F32)).astype(BF16)
    return jnp.concatenate([high, low], 0)


def placing(ids):
    ids_t = ids.astype(F32)
    expert_of = (iota((SLOTS, TOK), 0) // CAP).astype(F32)
    hit = jnp.zeros((SLOTS, TOK), F32)
    for k in range(TOP):
        hit = jnp.where(ids_t[k : k + 1, :] == expert_of, 1.0, hit)
    earlier = one_hot(iota((TOK, TOK), 0) < iota((TOK, TOK), 1))
    before = nn(hit.astype(BF16), earlier)
    turn = (iota((SLOTS, TOK), 0) % CAP).astype(F32)
    place = jnp.where(before == turn, hit, 0.0).astype(BF16)
    return place, nt(place, ids_t.astype(BF16))


def normalize(comp, gain):
    mean = jnp.mean(comp * comp, -1, keepdims=True)
    return (comp * lax.rsqrt(mean + 1e-06) * gain).astype(BF16)


def slot_weights(normed, router, slot_ids):
    scores = jax.nn.sigmoid(nn(normed, router))
    lane = iota((SLOTS, EXPERTS), 1)
    lane_f = lane.astype(F32)
    picked = jnp.zeros((SLOTS, EXPERTS), F32)
    for k in range(TOP):
        picked = jnp.where(slot_ids[:, k : k + 1] == lane_f, 1.0, picked)
    total = jnp.sum(scores * picked, -1, keepdims=True)
    own = jnp.sum(
        jnp.where(lane == iota((SLOTS, EXPERTS), 0) // CAP, scores, 0.0), -1, keepdims=True
    )
    return SCALE * own / total


def kernel(
    held, incoming, ids, gain, router, wg, wu, wd, out,
    xv, xp, idv, idp, gv, rv, wgu, wdv,
    zsend, zrecv, xa, xb, rsend, rrecv, guf, hbuf, oa, ob, pa, pb, of, bsend, brecv,
    wsend, wrecv, yv, b1, ov, comp_s, comp1_s,
    loc, snd, rcv,
):
    xbuf, osend, orecv = (xa, xb), (oa, ob), (pa, pb)
    sec = lax.axis_index("section")
    ex = lax.axis_index("expert")
    z, x = ex // SUB, ex % SUB
    e, zz = z // SUB, z % SUB

    def at_z(other):
        return {"expert": other * SUB + x}

    def at_x(other):
        return {"expert": z * SUB + other}

    def at_next(other):
        return {"section": (sec + 1) % NSEC, "expert": other * SUB + x}

    def at_previous(other):
        return {"section": (sec + NSEC - 1) % NSEC, "expert": other * SUB + x}

    after = at_next(z)

    flip = 1 - 2 * (sec % 2)

    def turn(k):
        step = jnp.where(k % 2 == 1, 8 - k // 2, k // 2 - 8)
        return (z + flip * step + NZ) % NZ

    def local(src, dst, number):
        return pltpu.make_async_copy(src, dst, loc.at[number])

    def send(src, dst, number, device):
        pltpu.make_async_remote_copy(
            src_ref=src, dst_ref=dst, send_sem=snd.at[number], recv_sem=rcv.at[number],
            device_id=device, device_id_type=MESH,
        ).start()

    def arrived(ref, number):
        pltpu.make_async_copy(ref, ref, rcv.at[number]).wait()

    def sent(ref, number):
        pltpu.make_async_copy(ref, ref, snd.at[number]).wait()

    barrier = pltpu.get_barrier_semaphore()

    @pl.loop(1, NZ)
    def _(k):
        pl.semaphore_signal(barrier, inc=1, device_id=at_z((z + k) % NZ), device_id_type=MESH)

    @pl.loop(0, NZ)
    def _(k):
        pl.semaphore_signal(barrier, inc=1, device_id=at_previous((z + k) % NZ), device_id_type=MESH)

    for k in range(1, SUB):
        pl.semaphore_signal(barrier, inc=1, device_id=at_x((x + k) % SUB), device_id_type=MESH)

    own = pl.ds(pl.multiple_of(zz * DS, 128), DS)
    starts = [
        local(held.at[0], xv, L_X),
        local(ids.at[:, 0], idv, L_IDS),
        local(gain, gv, L_GAIN),
        local(router.at[0], rv, L_ROUTER),
        local(wg.at[0, :, own], wgu.at[0, zz], L_WGU),
        local(wu.at[0, :, own], wgu.at[1, zz], L_WGU),
        local(wd.at[0, :, own], wdv.at[zz], L_WD),
    ]
    for copy in starts:
        copy.start()

    local(ids.at[:, 0], idv, L_IDS).wait()
    place0, slot_ids0 = placing(idv[0])
    pl.semaphore_wait(barrier, NZ - 1 + SUB - 1 + NZ)

    def exchange(source, target, number):
        for k in (2, 1, 3):
            to = (zz + k) % SUB
            columns = pl.ds(pl.multiple_of(to * DS, 128), DS)
            send(source.at[0, :, columns], target.at[zz], number, at_z(e * SUB + to))

    exchange(wg, wgu.at[0], S_WGU)
    local(gain, gv, L_GAIN).wait()
    gain_row = gv[...].astype(F32)
    local(held.at[0], xv, L_X).wait()
    low4 = iota((1, 8, 128), 1) < 4

    def pairs(get, zeros, half):
        evens, odds = [], []
        for v in range(2):
            block = BLOCKS[half][0] + 2 * v
            a = get(block)
            b = get(block + 1) if block + 1 < LB else zeros
            evens.append(jnp.where(low4, a, swap_halves(b)))
            odds.append(jnp.where(low4, swap_halves(a), b))
        return evens, odds

    def to_all_z(source, target, number, onward=False):
        @pl.loop(1, NZ)
        def _(k):
            to = turn(k)
            device = at_next(to) if onward else at_z(to)
            send(source.at[to // 2, to % 2], target.at[z], number, device)

        if onward:
            send(source.at[z // 2, z % 2], target.at[z], number, after)
        else:
            target[z] = source[z // 2, z % 2]

    def dispatch(tick, normed):
        rows = normed.astype(F32)
        for half in range(2):
            for part in range(SUB):

                def get(block):
                    column = (part * LB + block) * 128
                    return rows[:, column : column + 128].reshape(2, 8, 128)

                evens, odds = pairs(get, jnp.zeros((2, 8, 128), F32), half)
                even = jnp.concatenate(evens, 1).astype(BF16)
                odd = jnp.concatenate(odds, 1).astype(BF16)
                for h in range(2):
                    for n, message in ((2 * h, even[h]), (2 * h + 1, odd[h])):
                        to = n * SUB + part
                        zsend[tick, half, to // 2, to % 2] = message
            to_all_z(zsend.at[tick, half], zrecv.at[tick, half], S_TICK + PER_TICK * tick + half)

    def relay():
        @pl.when(sec == NSEC - 1)
        def _():
            send(incoming.at[0], xp, S_X, after)

        @pl.when(sec != NSEC - 1)
        def _():
            send(held.at[0], xp, S_X, after)

    def layer(tick, meanwhile, finish):
        base = S_TICK + PER_TICK * tick
        for half in range(2):
            arrived(zrecv.at[tick, half, pl.ds(0, NZ - 1)], base + half)
            got = zrecv[tick, half].astype(F32).reshape(8, 2, 2, 8, 128)
            mine = xbuf[half].at[tick, x]
            for v in range(2):
                a, b = got[:, 0, v], got[:, 1, v]
                even = jnp.where(low4, a, swap_halves(b))
                mine[:, 2 * v * 128 : (2 * v + 1) * 128] = even.reshape(64, 128).astype(BF16)
                if BLOCKS[half][0] + 2 * v + 1 < LB:
                    odd = jnp.where(low4, swap_halves(a), b)
                    mine[:, (2 * v + 1) * 128 : (2 * v + 2) * 128] = odd.reshape(64, 128).astype(BF16)
            for k in range(1, SUB):
                send(mine, mine, base + 2 + half, at_x((x + k) % SUB))
        if tick == 0:
            local(wgu.at[:, zz], wgu.at[:, zz], L_WGU).wait()
            arrived(wgu.at[:, pl.ds(0, SUB - 1)], S_WGU)
            exchange(wd, wdv, S_WD)
        arrived(xbuf[0].at[tick, pl.ds(0, SUB - 1)], base + 2)
        low, high = HALF[0]
        guf[...] = nt(xbuf[0][tick].reshape(256, 512), wgu[:, :, :, low:high].reshape(512, 512))
        arrived(xbuf[1].at[tick, pl.ds(0, SUB - 1)], base + 3)
        low, high = HALF[1]
        rows = xbuf[1][tick].reshape(256, DS - 512)
        for half in range(2):
            for which in range(2):
                weight = wgu[which, 2 * half : 2 * half + 2, :, low:high].reshape(128, DS - 512)
                column = which * 256 + half * 128
                sums = guf[:, column : column + 128] + nt(rows, weight)
                guf[:, column : column + 128] = sums
                rsend[tick, half, :, :, which * 128 : which * 128 + 128] = sums.reshape(SUB, 64, 128).astype(BF16)
            for k in range(1, SUB):
                to = (zz + k) % SUB
                send(rsend.at[tick, half, to], rrecv.at[tick, half, zz], base + 4 + half, at_z(e * SUB + to))
        if tick == 0:
            relay()
        mine = pl.ds(pl.multiple_of(zz * 64, 64), 64)
        for half in range(2):
            arrived(rrecv.at[tick, half, pl.ds(0, SUB - 1)], base + 4 + half)
            gate = guf[mine, half * 128 : half * 128 + 128]
            upper = guf[mine, 256 + half * 128 : 256 + half * 128 + 128]
            for k in range(1, SUB):
                other = rrecv[tick, half, (zz + k) % SUB].astype(F32)
                gate = gate + other[:, :128]
                upper = upper + other[:, 128:]
            hbuf[tick, half, zz] = (jax.nn.silu(gate) * upper).astype(BF16)
            for k in range(1, SUB):
                send(hbuf.at[tick, half, zz], hbuf.at[tick, half, zz], base + 6 + half, at_z(e * SUB + (zz + k) % SUB))
        if tick == 0:
            local(wd.at[0, :, own], wdv.at[zz], L_WD).wait()
            arrived(wdv.at[pl.ds(0, SUB - 1)], S_WD)
        for half in range(2):
            arrived(hbuf.at[tick, half, pl.ds(0, SUB - 1)], base + 6 + half)
        hidden = jnp.concatenate([hbuf[tick, 0].reshape(256, 128), hbuf[tick, 1].reshape(256, 128)], 1)
        for half in range(2):
            low, high = HALF[half]
            product = nn(hidden, wdv[:, :, low:high].reshape(256, high - low)).reshape(SUB, 64, high - low)
            osend[half][tick] = product.astype(BF16)
            of[:, :, low:high] = product
            for k in range(1, SUB):
                to = (x + k) % SUB
                send(osend[half].at[tick, to], orecv[half].at[tick, x], base + 8 + half, at_x(to))
        for half in range(2):
            low, high = HALF[half]
            arrived(orecv[half].at[tick, pl.ds(0, SUB - 1)], base + 8 + half)
            total = of[x, :, low:high]
            for k in range(1, SUB):
                total = total + orecv[half][tick, (x + k) % SUB].astype(F32)

            def get(block):
                column = block * 128 - low
                return total[:, column : column + 128].reshape(8, 8, 128)

            evens, odds = pairs(get, jnp.zeros((8, 8, 128), F32), half)
            bsend[tick, half, :, 0] = jnp.concatenate(evens, 1).astype(BF16)
            bsend[tick, half, :, 1] = jnp.concatenate(odds, 1).astype(BF16)
            to_all_z(bsend.at[tick, half], brecv.at[tick, half], base + 10 + half, tick == 0)
        meanwhile()
        for half in range(2):
            low, high = HALF[half]
            arrived(brecv.at[tick, half, pl.ds(0, NZ - tick)], base + 10 + half)
            for part in range(SUB):
                rows = [brecv[tick, half, n * SUB + part].astype(F32).reshape(2, 8, 128) for n in range(4)]
                blocks = []
                for v in range(2):
                    top = [jnp.where(low4[0], rows[2 * h][v], swap_halves(rows[2 * h + 1][v])) for h in range(2)]
                    blocks.append(jnp.concatenate(top, 0))
                    if BLOCKS[half][0] + 2 * v + 1 < LB:
                        top = [jnp.where(low4[0], swap_halves(rows[2 * h][v]), rows[2 * h + 1][v]) for h in range(2)]
                        blocks.append(jnp.concatenate(top, 0))
                finish(half, part, slice(part * DS + low, part * DS + high), jnp.concatenate(blocks, 1))

    normed = normalize(nn(place0, xv[...]), gain_row)
    dispatch(0, normed)
    exchange(wu, wgu.at[1], S_WGU)
    send(idv.at[0], idp, S_IDS, after)
    local(router.at[0], rv, L_ROUTER).wait()
    wsend[...] = jnp.broadcast_to(slot_weights(normed, rv[...], slot_ids0), (SLOTS, 128))
    send(wsend, wrecv, S_Y, after)
    place1, slot_ids1 = placing(idv[1])
    known = {}

    def prepare():
        arrived(idp, S_IDS)
        prev, _ = placing(idp[...])
        lower = one_hot(iota((SLOTS, SLOTS), 1) < iota((SLOTS, SLOTS), 0))
        live = jnp.where(sec == 0, 0.0, 1.0)
        unique = jnp.where(nn(lower, prev) == 0.0, prev.astype(F32), 0.0) * live
        touched = jnp.sum(unique, 0, keepdims=True)
        untouched = (place1.astype(F32) * (1.0 - touched)).astype(BF16)
        unique = unique.astype(BF16)
        known["moved"] = nt(place1, unique).astype(BF16)
        eye = one_hot(iota((TOK, TOK), 0) == iota((TOK, TOK), 1))
        known["scatter"] = nt(eye, unique).astype(BF16)
        known["combine"] = nt(eye, jnp.concatenate([place1, place1], 0)).astype(BF16)
        known["kept"] = 1.0 - jnp.sum(known["scatter"].astype(F32), 1, keepdims=True)
        same = nt(prev, prev).astype(BF16)
        known["same"] = jnp.concatenate([same, same], 1)
        arrived(wrecv, S_Y)
        known["weights"] = wrecv[:, :1]
        arrived(xp, S_X)
        comp_s[...] = nn(prev, xp[...])
        comp1_s[...] = nn(untouched, xp[...])

    def changed(half, part, columns, moe):
        rows = comp_s[:, columns] + nn(known["same"], halves(moe * known["weights"]))
        yv[:, columns] = rows.astype(BF16)
        comp1_s[:, columns] += nn(known["moved"], yv[:, columns])

    layer(0, prepare, changed)
    kept, scatter, combine = known["kept"], known["scatter"], known["combine"]
    normed = normalize(comp1_s[...], gain_row)
    dispatch(1, normed)
    weights1 = slot_weights(normed, rv[...], slot_ids1)

    def block():
        for part in range(SUB):
            columns = slice(part * DS, (part + 1) * DS)
            b1[:, columns] = xp[:, columns].astype(F32) * kept + nn(scatter, yv[:, columns])

    outs = []

    def result(half, part, columns, moe):
        ov[:, columns] = (b1[:, columns] + nn(combine, halves(moe * weights1))).astype(BF16)
        copy = local(ov.at[:, columns], out.at[0, :, columns], L_OUT + SUB * half + part)
        copy.start()
        outs.append(copy)

    layer(1, block, result)
    sent(wgu.at[:, pl.ds(0, SUB - 1)], S_WGU)
    sent(wdv.at[pl.ds(0, SUB - 1)], S_WD)
    sent(xp, S_X)
    sent(idp, S_IDS)
    sent(wrecv, S_Y)
    for half in range(2):
        for tick in range(2):
            base = S_TICK + PER_TICK * tick + half
            sent(zrecv.at[tick, half, pl.ds(0, NZ - 1)], base)
            sent(xbuf[half].at[tick, pl.ds(0, SUB - 1)], base + 2)
            sent(rrecv.at[tick, half, pl.ds(0, SUB - 1)], base + 4)
            sent(hbuf.at[tick, half, pl.ds(0, SUB - 1)], base + 6)
            sent(orecv[half].at[tick, pl.ds(0, SUB - 1)], base + 8)
            sent(brecv.at[tick, half, pl.ds(0, NZ - tick)], base + 10)
    for copy in outs:
        copy.wait()


def body(held, incoming, route_ids, gain, router, w_gate, w_up, w_down):
    any_space = pl.BlockSpec(memory_space=pltpu.HBM)
    vm = pltpu.VMEM
    return pl.pallas_call(
        kernel,
        out_shape=jax.ShapeDtypeStruct((1, TOK, D), BF16),
        in_specs=[any_space] * 8,
        out_specs=any_space,
        scratch_shapes=[
            vm((TOK, D), BF16),
            vm((TOK, D), BF16),
            vm((2, TOP, TOK), jnp.int32),
            vm((TOP, TOK), jnp.int32),
            vm((1, D), BF16),
            vm((D, EXPERTS), BF16),
            vm((2, SUB, UNITS, DS), BF16),
            vm((SUB, UNITS, DS), BF16),
            vm((2, 2, 8, 2, 16, 128), BF16),
            vm((2, 2, NZ, 16, 128), BF16),
            vm((2, SUB, 64, 512), BF16),
            vm((2, SUB, 64, DS - 512), BF16),
            vm((2, 2, SUB, 64, 256), BF16),
            vm((2, 2, SUB, 64, 256), BF16),
            vm((256, 512), F32),
            vm((2, 2, SUB, 64, 128), BF16),
            vm((2, SUB, 64, 512), BF16),
            vm((2, SUB, 64, DS - 512), BF16),
            vm((2, SUB, 64, 512), BF16),
            vm((2, SUB, 64, DS - 512), BF16),
            vm((SUB, 64, DS), F32),
            vm((2, 2, 8, 2, 16, 128), BF16),
            vm((2, 2, NZ, 16, 128), BF16),
            vm((SLOTS, 128), F32),
            vm((SLOTS, 128), F32),
            vm((SLOTS, D), BF16),
            vm((TOK, D), F32),
            vm((TOK, D), BF16),
            vm((SLOTS, D), F32),
            vm((SLOTS, D), F32),
            pltpu.SemaphoreType.DMA((L_OUT + 2 * SUB,)),
            pltpu.SemaphoreType.DMA((N_SEM,)),
            pltpu.SemaphoreType.DMA((N_SEM,)),
        ],
        compiler_params=pltpu.CompilerParams(
            collective_id=0, has_side_effects=True, vmem_limit_bytes=60 * 1024 * 1024
        ),
    )(held, incoming, jnp.swapaxes(route_ids, 2, 3), gain, router, w_gate, w_up, w_down)


def solution(mesh):
    return jax.shard_map(
        body,
        mesh=mesh,
        in_specs=(
            P("section", "expert", None),
            P(None, "expert", None),
            P(None, "section", "expert", None),
            P("section", None),
            P("section", None, None),
            P("section", "expert", None),
            P("section", "expert", None),
            P("section", "expert", None),
        ),
        out_specs=P("section", "expert", None),
        check_vma=False,
    )
```

```python
import jax
import jax.numpy as jnp
from jax import lax
from jax.experimental import pallas as pl
from jax.experimental.pallas import tpu as pltpu
from jax.sharding import PartitionSpec as P

MESH = pl.DeviceIdType.MESH
F32 = jnp.float32
BF16 = jnp.bfloat16

SCALE = 2.5
D = 3584
TOK = 128
TOP = 8
CAP = 4
SLOTS = 16
UNITS = 64
NZ = 16
SUB = 4
DS = D // SUB
LB = DS // 128
EXPERTS = 256
HALF = (0, 512), (512, DS)
BLOCKS = (0, 4), (4, LB)
NSEC = 16

S_WGU, S_WD, S_X, S_IDS, S_Y = 1, 2, 3, 4, 5
S_TICK = 7
PER_TICK = 12
N_SEM = S_TICK + 2 * PER_TICK
L_X, L_IDS, L_GAIN, L_ROUTER, L_WGU, L_WD, L_OUT = range(7)


def nt(a, b):
    return lax.dot_general(a, b, (((1,), (1,)), ((), ())), preferred_element_type=F32)


def nn(a, b):
    return jnp.dot(a, b, preferred_element_type=F32)


def iota(shape, dim):
    return lax.broadcasted_iota(jnp.int32, shape, dim)


def swap_halves(a):
    return pltpu.roll(a, 4, a.ndim - 2)


def one_hot(flag):
    return jnp.where(flag, 1.0, 0.0).astype(BF16)


def halves(a):
    high = a.astype(BF16)
    low = (a - high.astype(F32)).astype(BF16)
    return jnp.concatenate([high, low], 0)


def placing(ids):
    ids_t = ids.astype(F32)
    expert_of = (iota((SLOTS, TOK), 0) // CAP).astype(F32)
    hit = jnp.zeros((SLOTS, TOK), F32)
    for k in range(TOP):
        hit = jnp.where(ids_t[k : k + 1, :] == expert_of, 1.0, hit)
    earlier = one_hot(iota((TOK, TOK), 0) < iota((TOK, TOK), 1))
    before = nn(hit.astype(BF16), earlier)
    turn = (iota((SLOTS, TOK), 0) % CAP).astype(F32)
    place = jnp.where(before == turn, hit, 0.0).astype(BF16)
    return place, nt(place, ids_t.astype(BF16))


def normalize(comp, gain):
    mean = jnp.mean(comp * comp, -1, keepdims=True)
    return (comp * lax.rsqrt(mean + 1e-06) * gain).astype(BF16)


def slot_weights(normed, router, slot_ids):
    scores = jax.nn.sigmoid(nn(normed, router))
    lane = iota((SLOTS, EXPERTS), 1)
    lane_f = lane.astype(F32)
    picked = jnp.zeros((SLOTS, EXPERTS), F32)
    for k in range(TOP):
        picked = jnp.where(slot_ids[:, k : k + 1] == lane_f, 1.0, picked)
    total = jnp.sum(scores * picked, -1, keepdims=True)
    own = jnp.sum(
        jnp.where(lane == iota((SLOTS, EXPERTS), 0) // CAP, scores, 0.0), -1, keepdims=True
    )
    return SCALE * own / total


def kernel(
    held, incoming, ids, gain, router, wg, wu, wd, out,
    xv, xp, idv, idp, gv, rv, wgu, wdv,
    zsend, zrecv, xa, xb, rsend, rrecv, guf, hbuf, oa, ob, pa, pb, of, bsend, brecv,
    wsend, wrecv, yv, b1, ov, comp_s, comp1_s,
    loc, snd, rcv,
):
    xbuf, osend, orecv = (xa, xb), (oa, ob), (pa, pb)
    sec = lax.axis_index("section")
    ex = lax.axis_index("expert")
    z, x = ex // SUB, ex % SUB
    e, zz = z // SUB, z % SUB

    def at_z(other):
        return {"expert": other * SUB + x}

    def at_x(other):
        return {"expert": z * SUB + other}

    def at_next(other):
        return {"section": (sec + 1) % NSEC, "expert": other * SUB + x}

    def at_previous(other):
        return {"section": (sec + NSEC - 1) % NSEC, "expert": other * SUB + x}

    after = at_next(z)

    flip = 1 - 2 * (sec % 2)
    far_first = 2, 2 - flip, 2 + flip

    def turn(k):
        step = jnp.where(k % 2 == 1, 8 - k // 2, k // 2 - 8)
        return (z + flip * step + NZ) % NZ

    def local(src, dst, number):
        return pltpu.make_async_copy(src, dst, loc.at[number])

    def send(src, dst, number, device):
        pltpu.make_async_remote_copy(
            src_ref=src, dst_ref=dst, send_sem=snd.at[number], recv_sem=rcv.at[number],
            device_id=device, device_id_type=MESH,
        ).start()

    def arrived(ref, number):
        pltpu.make_async_copy(ref, ref, rcv.at[number]).wait()

    def sent(ref, number):
        pltpu.make_async_copy(ref, ref, snd.at[number]).wait()

    barrier = pltpu.get_barrier_semaphore()

    @pl.loop(1, NZ)
    def _(k):
        pl.semaphore_signal(barrier, inc=1, device_id=at_z((z + k) % NZ), device_id_type=MESH)

    @pl.loop(0, NZ)
    def _(k):
        pl.semaphore_signal(barrier, inc=1, device_id=at_previous((z + k) % NZ), device_id_type=MESH)

    for k in range(1, SUB):
        pl.semaphore_signal(barrier, inc=1, device_id=at_x((x + k) % SUB), device_id_type=MESH)

    own = pl.ds(pl.multiple_of(zz * DS, 128), DS)
    starts = [
        local(held.at[0], xv, L_X),
        local(ids.at[:, 0], idv, L_IDS),
        local(gain, gv, L_GAIN),
        local(router.at[0], rv, L_ROUTER),
        local(wg.at[0, :, own], wgu.at[0, zz], L_WGU),
        local(wu.at[0, :, own], wgu.at[1, zz], L_WGU),
        local(wd.at[0, :, own], wdv.at[zz], L_WD),
    ]
    for copy in starts:
        copy.start()

    local(ids.at[:, 0], idv, L_IDS).wait()
    place0, slot_ids0 = placing(idv[0])
    pl.semaphore_wait(barrier, NZ - 1 + SUB - 1 + NZ)

    def exchange(source, target, number):
        for k in (2, 1, 3):
            to = (zz + k) % SUB
            columns = pl.ds(pl.multiple_of(to * DS, 128), DS)
            send(source.at[0, :, columns], target.at[zz], number, at_z(e * SUB + to))

    exchange(wg, wgu.at[0], S_WGU)
    local(gain, gv, L_GAIN).wait()
    gain_row = gv[...].astype(F32)
    local(held.at[0], xv, L_X).wait()
    low4 = iota((1, 8, 128), 1) < 4

    def pairs(get, zeros, half):
        evens, odds = [], []
        for v in range(2):
            block = BLOCKS[half][0] + 2 * v
            a = get(block)
            b = get(block + 1) if block + 1 < LB else zeros
            evens.append(jnp.where(low4, a, swap_halves(b)))
            odds.append(jnp.where(low4, swap_halves(a), b))
        return evens, odds

    def to_all_z(source, target, number, onward=False):
        @pl.loop(1, NZ)
        def _(k):
            to = turn(k)
            device = at_next(to) if onward else at_z(to)
            send(source.at[to // 2, to % 2], target.at[z], number, device)

        if onward:
            send(source.at[z // 2, z % 2], target.at[z], number, after)
        else:
            target[z] = source[z // 2, z % 2]

    def dispatch(tick, normed):
        rows = normed.astype(F32)
        for half in range(2):
            for part in range(SUB):

                def get(block):
                    column = (part * LB + block) * 128
                    return rows[:, column : column + 128].reshape(2, 8, 128)

                evens, odds = pairs(get, jnp.zeros((2, 8, 128), F32), half)
                even = jnp.concatenate(evens, 1).astype(BF16)
                odd = jnp.concatenate(odds, 1).astype(BF16)
                for h in range(2):
                    for n, message in ((2 * h, even[h]), (2 * h + 1, odd[h])):
                        to = n * SUB + part
                        zsend[tick, half, to // 2, to % 2] = message
            to_all_z(zsend.at[tick, half], zrecv.at[tick, half], S_TICK + PER_TICK * tick + half)

    def relay():
        @pl.when(sec == NSEC - 1)
        def _():
            send(incoming.at[0], xp, S_X, after)

        @pl.when(sec != NSEC - 1)
        def _():
            send(held.at[0], xp, S_X, after)

    def layer(tick, meanwhile, later, finish):
        base = S_TICK + PER_TICK * tick
        for half in range(2):
            arrived(zrecv.at[tick, half, pl.ds(0, NZ - 1)], base + half)
            got = zrecv[tick, half].astype(F32).reshape(8, 2, 2, 8, 128)
            mine = xbuf[half].at[tick, x]
            for v in range(2):
                a, b = got[:, 0, v], got[:, 1, v]
                even = jnp.where(low4, a, swap_halves(b))
                mine[:, 2 * v * 128 : (2 * v + 1) * 128] = even.reshape(64, 128).astype(BF16)
                if BLOCKS[half][0] + 2 * v + 1 < LB:
                    odd = jnp.where(low4, swap_halves(a), b)
                    mine[:, (2 * v + 1) * 128 : (2 * v + 2) * 128] = odd.reshape(64, 128).astype(BF16)
            for k in far_first:
                send(mine, mine, base + 2 + half, at_x((x + k) % SUB))
        if tick == 0:
            local(wgu.at[:, zz], wgu.at[:, zz], L_WGU).wait()
            arrived(wgu.at[:, pl.ds(0, SUB - 1)], S_WGU)
        arrived(xbuf[0].at[tick, pl.ds(0, SUB - 1)], base + 2)
        low, high = HALF[0]
        guf[...] = nt(xbuf[0][tick].reshape(256, 512), wgu[:, :, :, low:high].reshape(512, 512))
        arrived(xbuf[1].at[tick, pl.ds(0, SUB - 1)], base + 3)
        low, high = HALF[1]
        rows = xbuf[1][tick].reshape(256, DS - 512)
        for half in range(2):
            for which in range(2):
                weight = wgu[which, 2 * half : 2 * half + 2, :, low:high].reshape(128, DS - 512)
                column = which * 256 + half * 128
                sums = guf[:, column : column + 128] + nt(rows, weight)
                guf[:, column : column + 128] = sums
                rsend[tick, half, :, :, which * 128 : which * 128 + 128] = sums.reshape(SUB, 64, 128).astype(BF16)
            for k in far_first:
                to = (zz + k) % SUB
                send(rsend.at[tick, half, to], rrecv.at[tick, half, zz], base + 4 + half, at_z(e * SUB + to))
        if tick == 0:
            relay()
        mine = pl.ds(pl.multiple_of(zz * 64, 64), 64)
        for half in range(2):
            arrived(rrecv.at[tick, half, pl.ds(0, SUB - 1)], base + 4 + half)
            gate = guf[mine, half * 128 : half * 128 + 128]
            upper = guf[mine, 256 + half * 128 : 256 + half * 128 + 128]
            for k in range(1, SUB):
                other = rrecv[tick, half, (zz + k) % SUB].astype(F32)
                gate = gate + other[:, :128]
                upper = upper + other[:, 128:]
            hbuf[tick, half, zz] = (jax.nn.silu(gate) * upper).astype(BF16)
            for k in far_first:
                send(hbuf.at[tick, half, zz], hbuf.at[tick, half, zz], base + 6 + half, at_z(e * SUB + (zz + k) % SUB))
        if tick == 0:
            local(wd.at[0, :, own], wdv.at[zz], L_WD).wait()
            arrived(wdv.at[pl.ds(0, SUB - 1)], S_WD)
        for half in range(2):
            arrived(hbuf.at[tick, half, pl.ds(0, SUB - 1)], base + 6 + half)
        hidden = jnp.concatenate([hbuf[tick, 0].reshape(256, 128), hbuf[tick, 1].reshape(256, 128)], 1)
        for half in range(2):
            low, high = HALF[half]
            product = nn(hidden, wdv[:, :, low:high].reshape(256, high - low)).reshape(SUB, 64, high - low)
            osend[half][tick] = product.astype(BF16)
            of[:, :, low:high] = product
            for k in far_first:
                to = (x + k) % SUB
                send(osend[half].at[tick, to], orecv[half].at[tick, x], base + 8 + half, at_x(to))
        meanwhile()
        for half in range(2):
            low, high = HALF[half]
            arrived(orecv[half].at[tick, pl.ds(0, SUB - 1)], base + 8 + half)
            total = of[x, :, low:high]
            for k in range(1, SUB):
                total = total + orecv[half][tick, (x + k) % SUB].astype(F32)

            def get(block):
                column = block * 128 - low
                return total[:, column : column + 128].reshape(8, 8, 128)

            evens, odds = pairs(get, jnp.zeros((8, 8, 128), F32), half)
            bsend[tick, half, :, 0] = jnp.concatenate(evens, 1).astype(BF16)
            bsend[tick, half, :, 1] = jnp.concatenate(odds, 1).astype(BF16)
            to_all_z(bsend.at[tick, half], brecv.at[tick, half], base + 10 + half, tick == 0)
        later()
        for half in range(2):
            low, high = HALF[half]
            arrived(brecv.at[tick, half, pl.ds(0, NZ - tick)], base + 10 + half)
            for part in range(SUB):
                rows = [brecv[tick, half, n * SUB + part].astype(F32).reshape(2, 8, 128) for n in range(4)]
                blocks = []
                for v in range(2):
                    top = [jnp.where(low4[0], rows[2 * h][v], swap_halves(rows[2 * h + 1][v])) for h in range(2)]
                    blocks.append(jnp.concatenate(top, 0))
                    if BLOCKS[half][0] + 2 * v + 1 < LB:
                        top = [jnp.where(low4[0], swap_halves(rows[2 * h][v]), rows[2 * h + 1][v]) for h in range(2)]
                        blocks.append(jnp.concatenate(top, 0))
                finish(half, part, slice(part * DS + low, part * DS + high), jnp.concatenate(blocks, 1))

    normed = normalize(nn(place0, xv[...]), gain_row)
    dispatch(0, normed)
    exchange(wu, wgu.at[1], S_WGU)
    exchange(wd, wdv, S_WD)
    send(idv.at[0], idp, S_IDS, after)
    local(router.at[0], rv, L_ROUTER).wait()
    wsend[...] = jnp.broadcast_to(slot_weights(normed, rv[...], slot_ids0), (SLOTS, 128))
    send(wsend, wrecv, S_Y, after)
    place1, slot_ids1 = placing(idv[1])

    arrived(idp, S_IDS)
    prev, _ = placing(idp[...])
    lower = one_hot(iota((SLOTS, SLOTS), 1) < iota((SLOTS, SLOTS), 0))
    live = jnp.where(sec == 0, 0.0, 1.0)
    unique = jnp.where(nn(lower, prev) == 0.0, prev.astype(F32), 0.0) * live
    touched = jnp.sum(unique, 0, keepdims=True)
    untouched = (place1.astype(F32) * (1.0 - touched)).astype(BF16)
    unique = unique.astype(BF16)
    moved = nt(place1, unique).astype(BF16)
    eye = one_hot(iota((TOK, TOK), 0) == iota((TOK, TOK), 1))
    scatter = nt(eye, unique).astype(BF16)
    combine = nt(eye, jnp.concatenate([place1, place1], 0)).astype(BF16)
    kept = 1.0 - jnp.sum(scatter.astype(F32), 1, keepdims=True)
    same = nt(prev, prev).astype(BF16)
    same = jnp.concatenate([same, same], 1)

    def prepare():
        arrived(xp, S_X)
        both = nn(jnp.concatenate([prev, untouched], 0), xp[...])
        comp_s[...] = both[:SLOTS]
        comp1_s[...] = both[SLOTS:]
        arrived(wrecv, S_Y)

    def changed(half, part, columns, moe):
        rows = comp_s[:, columns] + nn(same, halves(moe * wrecv[:, :1]))
        yv[:, columns] = rows.astype(BF16)
        comp1_s[:, columns] += nn(moved, yv[:, columns])

    layer(0, prepare, lambda: None, changed)
    normed = normalize(comp1_s[...], gain_row)
    dispatch(1, normed)
    weights1 = slot_weights(normed, rv[...], slot_ids1)

    def block():
        for part in range(SUB):
            columns = slice(part * DS, (part + 1) * DS)
            b1[:, columns] = xp[:, columns].astype(F32) * kept + nn(scatter, yv[:, columns])

    outs = []

    def result(half, part, columns, moe):
        ov[:, columns] = (b1[:, columns] + nn(combine, halves(moe * weights1))).astype(BF16)
        copy = local(ov.at[:, columns], out.at[0, :, columns], L_OUT + SUB * half + part)
        copy.start()
        outs.append(copy)

    layer(1, block, lambda: None, result)
    sent(wgu.at[:, pl.ds(0, SUB - 1)], S_WGU)
    sent(wdv.at[pl.ds(0, SUB - 1)], S_WD)
    sent(xp, S_X)
    sent(idp, S_IDS)
    sent(wrecv, S_Y)
    for half in range(2):
        for tick in range(2):
            base = S_TICK + PER_TICK * tick + half
            sent(zrecv.at[tick, half, pl.ds(0, NZ - 1)], base)
            sent(xbuf[half].at[tick, pl.ds(0, SUB - 1)], base + 2)
            sent(rrecv.at[tick, half, pl.ds(0, SUB - 1)], base + 4)
            sent(hbuf.at[tick, half, pl.ds(0, SUB - 1)], base + 6)
            sent(orecv[half].at[tick, pl.ds(0, SUB - 1)], base + 8)
            sent(brecv.at[tick, half, pl.ds(0, NZ - tick)], base + 10)
    for copy in outs:
        copy.wait()


def body(held, incoming, route_ids, gain, router, w_gate, w_up, w_down):
    any_space = pl.BlockSpec(memory_space=pltpu.HBM)
    vm = pltpu.VMEM
    return pl.pallas_call(
        kernel,
        out_shape=jax.ShapeDtypeStruct((1, TOK, D), BF16),
        in_specs=[any_space] * 8,
        out_specs=any_space,
        scratch_shapes=[
            vm((TOK, D), BF16),
            vm((TOK, D), BF16),
            vm((2, TOP, TOK), jnp.int32),
            vm((TOP, TOK), jnp.int32),
            vm((1, D), BF16),
            vm((D, EXPERTS), BF16),
            vm((2, SUB, UNITS, DS), BF16),
            vm((SUB, UNITS, DS), BF16),
            vm((2, 2, 8, 2, 16, 128), BF16),
            vm((2, 2, NZ, 16, 128), BF16),
            vm((2, SUB, 64, 512), BF16),
            vm((2, SUB, 64, DS - 512), BF16),
            vm((2, 2, SUB, 64, 256), BF16),
            vm((2, 2, SUB, 64, 256), BF16),
            vm((256, 512), F32),
            vm((2, 2, SUB, 64, 128), BF16),
            vm((2, SUB, 64, 512), BF16),
            vm((2, SUB, 64, DS - 512), BF16),
            vm((2, SUB, 64, 512), BF16),
            vm((2, SUB, 64, DS - 512), BF16),
            vm((SUB, 64, DS), F32),
            vm((2, 2, 8, 2, 16, 128), BF16),
            vm((2, 2, NZ, 16, 128), BF16),
            vm((SLOTS, 128), F32),
            vm((SLOTS, 128), F32),
            vm((SLOTS, D), BF16),
            vm((TOK, D), F32),
            vm((TOK, D), BF16),
            vm((SLOTS, D), F32),
            vm((SLOTS, D), F32),
            pltpu.SemaphoreType.DMA((L_OUT + 2 * SUB,)),
            pltpu.SemaphoreType.DMA((N_SEM,)),
            pltpu.SemaphoreType.DMA((N_SEM,)),
        ],
        compiler_params=pltpu.CompilerParams(
            collective_id=0, has_side_effects=True, vmem_limit_bytes=60 * 1024 * 1024
        ),
    )(held, incoming, jnp.swapaxes(route_ids, 2, 3), gain, router, w_gate, w_up, w_down)


def solution(mesh):
    return jax.shard_map(
        body,
        mesh=mesh,
        in_specs=(
            P("section", "expert", None),
            P(None, "expert", None),
            P(None, "section", "expert", None),
            P("section", None),
            P("section", None, None),
            P("section", "expert", None),
            P("section", "expert", None),
            P("section", "expert", None),
        ),
        out_specs=P("section", "expert", None),
        check_vma=False,
    )
```
